1024 devices in a mesh: owner: 256 (over x, z, core), shard: 4 (over y).
Axes of the slice: x: 4, y: 4, z: 32, core: 2. Of those that a mesh axis runs over, the one named last changes fastest.
Arguments:
- grad_rows: bfloat16 [256, 512, 512], P('owner', 'shard'), may hold values from -6 to 6
- owner_list: int32 [256], replicated, may hold values from 3 to 255, as said below
- basis_left: float32 [512, 512, 512], P('owner'), may hold values from -0.25 to 0.25
- basis_right: float32 [512, 512, 512], P('owner'), may hold values from -0.25 to 0.25
- first_moment: float32 [512, 512, 512], P('owner', 'shard'), may hold values from -3 to 3
- second_moment: float32 [512, 512, 512], P('owner', 'shard'), may hold values from 0.01 to 0.1
Outputs:
- update: bfloat16 [256, 512, 512], P('owner', 'shard')
- new_first: float32 [512, 512, 512], P('owner', 'shard')
- new_second: float32 [512, 512, 512], P('owner', 'shard')
The draws below stay inside these ranges and needn't reach their ends.
Inputs may be any that keep to these rules, and one draw needn't show every extreme that they name: `owner_list`: the list never falls; block b's owner lies among groups b to b + 3; no group owns more than 2 blocks, and in every draw some group owns 2 and some block's owner is 3 groups after it.
All inputs are finite; a program needn't handle non-finite values.
Results may differ from the reference program's by a relative error of at most 0.009.
Values may be sent and summed in bfloat16 or wider, within the bound.
No kernel may reach another device: no remote copies, remote signals or barrier semaphores. Data moves between devices by JAX's collectives and lax.ppermute only.
A program may use at most 32 MiB of HBM per device.

```python
import math
import jax
import jax.numpy as jnp
from jax import lax

B = 512
CAP = 2
REACH = 4
BLOCKS = 256
SLOTS = 512


def draw_owner_list(key, part):
    key = jax.random.fold_in(key, 7)
    second_key = jax.random.fold_in(key, 1)
    forced = jnp.int32(0)
    wishes = jax.random.randint(second_key, (BLOCKS,), 0, CAP + 1).astype(jnp.int32)
    positions = jnp.arange(BLOCKS, dtype=jnp.int32)

    def advance(lag, inputs):
        position, wish = inputs
        upper = jnp.minimum(CAP, lag + 1)
        lower = jnp.maximum(0, lag + 1 - jnp.minimum(REACH - 1, BLOCKS - position - 1))
        load = jnp.clip(wish, lower, upper)
        quiet = (position >= forced) & (position < forced + REACH - 1)
        load = jnp.where(quiet, lower, load)
        load = jnp.where(position == forced + REACH - 1, upper, load)
        load = load.astype(jnp.int32)
        return ((lag + 1 - load).astype(jnp.int32), load)
    final_lag, loads = lax.scan(advance, jnp.int32(0), (positions, wishes))
    ends = jnp.cumsum(loads).astype(jnp.int32)
    return jnp.sum((ends[None, :] <= positions[:, None]).astype(jnp.int32), axis=1).astype(jnp.int32)


def level_of(stream_key, extent, cuts, smallest, high):
    def one(dim, parts):
        draws = jax.random.uniform(jax.random.fold_in(jax.random.fold_in(stream_key, 6), dim), (parts,), jnp.float32, smallest / len(cuts), high / len(cuts))
        return jnp.repeat(jnp.exp(draws), extent[dim] // parts).reshape((-1,) + (1,) * (len(extent) - dim - 1))

    loudness = one(*cuts[0])
    for cut in cuts[1:]:
        loudness = loudness * one(*cut)
    return loudness


def centred(stream_key, dims, deviation, limit, shards=(), held_as=jnp.bfloat16):
    values = jax.random.normal(stream_key, dims, jnp.float32) * deviation
    if len(shards) > 0:
        values = level_of(stream_key, dims, shards, -0.22, 0.18) * values
    return jnp.clip(values, min=-limit, max=limit).astype(held_as)


def setup_inputs(seed: int = 0) -> dict:
    arg_keys = jax.random.split(jax.random.key(seed), 7)
    return {
        "grad_rows": centred(arg_keys[0], (BLOCKS, B, B), 1.0, 6.0, ((0, 256), (1, 4))),
        "owner_list": draw_owner_list(jax.random.fold_in(arg_keys[6], 71), 0),
        "basis_left": centred(arg_keys[2], (SLOTS, B, B), B ** -0.5, 0.25, ((0, 256),), jnp.float32),
        "basis_right": centred(arg_keys[3], (SLOTS, B, B), B ** -0.5, 0.25, ((0, 256),), jnp.float32),
        "first_moment": centred(arg_keys[4], (SLOTS, B, B), 0.5, 3.0, ((0, 256), (1, 4)), jnp.float32),
        "second_moment": jnp.clip(jnp.exp(math.log(0.1) - 2.3025851 * jax.random.uniform(arg_keys[5], (SLOTS, B, B), jnp.float32) ** level_of(arg_keys[5], (SLOTS, B, B), ((0, 256), (1, 4)), -0.2, 0.2)), 0.01, 0.1),
    }


beta_first = 0.9
beta_second = 0.999
epsilon = 1e-08

def matmul(left_side, right_side):
    return jnp.dot(left_side, right_side, preferred_element_type=jnp.float32, precision=lax.Precision.HIGHEST)

def reference(grad_rows, owner_list, basis_left, basis_right, first_moment, second_moment):
    block_count = grad_rows.shape[0]
    order = jnp.arange(block_count, dtype=jnp.int32)
    same_owner = owner_list[None, :] == owner_list[:, None]
    rank_in = lax.optimization_barrier(jnp.sum((same_owner & (order[None, :] < order[:, None])).astype(jnp.int32), axis=1)).astype(jnp.int32)
    slot_of = (owner_list * CAP + rank_in).astype(jnp.int32)
    slot_hit = slot_of[None, :] == jnp.arange(SLOTS, dtype=jnp.int32)[:, None]
    slot_used = jnp.any(slot_hit, axis=1)
    slot_block = lax.optimization_barrier(jnp.sum(jnp.where(slot_hit, order[None, :], 0), axis=1)).astype(jnp.int32)

    def one_slot(inputs):
        left_basis, right_basis, first, second, picked, is_live = inputs
        gradient = jnp.where(is_live, grad_rows[picked].astype(jnp.float32), jnp.float32(0.0))
        inner = matmul(left_basis.T, gradient)
        rotated = matmul(inner, right_basis)
        fresh_first = beta_first * first + (1.0 - beta_first) * rotated
        fresh_second = beta_second * second + (1.0 - beta_second) * rotated * rotated
        direction = fresh_first / (jnp.sqrt(fresh_second) + epsilon)
        tail = matmul(direction, right_basis.T)
        turned = matmul(left_basis, tail)
        return (turned, fresh_first, fresh_second)
    turned, new_first, new_second = lax.map(one_slot, (basis_left, basis_right, first_moment, second_moment, slot_block, slot_used))
    update = turned[slot_of].astype(jnp.bfloat16)
    return (update, new_first, new_second)
```

```python
import functools

import jax
import jax.numpy as jnp
from jax import lax
from jax.experimental import pallas as pl
from jax.experimental.pallas import tpu as pltpu
from jax.sharding import PartitionSpec as P

REACH = 4
CAP = 2

beta_first = 0.9
beta_second = 0.999
epsilon = 1e-08
bf16 = jnp.bfloat16
f32 = jnp.float32
VMEM = pl.BlockSpec(memory_space=pltpu.VMEM)
SMEM = pl.BlockSpec(memory_space=pltpu.SMEM)


def shifted(x, axis, by, wrap):
    devices = lax.axis_size(axis)
    if wrap:
        pairs = [(i, (i + by) % devices) for i in range(devices)]
    else:
        pairs = [(i, i + by) for i in range(devices) if 0 <= i + by < devices]
    return lax.ppermute(x, axis, pairs)


def rank_of(owner_ref, block):
    before = owner_ref[jnp.maximum(block - 1, 0)]
    return ((block > 0) & (before == owner_ref[block])).astype(jnp.int32)


def split(x):
    high = x.astype(bf16)
    return high, (x - high.astype(f32)).astype(bf16)


def prepare(spot_ref, left_ref, right_ref, cols_ref, rows_ref, rights_ref):
    shard = spot_ref[1]
    own = pl.ds(pl.multiple_of(shard * 128, 128), 128)
    for slot in range(CAP):
        for step in range(4):
            peer = lax.rem(shard + 4 - step, 4)
            theirs = pl.ds(pl.multiple_of(peer * 128, 128), 128)
            here = slice(step * 128, (step + 1) * 128)
            high, low = split(left_ref[slot, theirs, own].T)
            cols_ref[0, slot, :, here] = high
            cols_ref[1, slot, :, here] = low
            high, low = split(left_ref[slot, own, theirs])
            rows_ref[0, slot, :, here] = high
            rows_ref[1, slot, :, here] = low
        high, low = split(right_ref[slot])
        rights_ref[0, slot] = high
        rights_ref[1, slot] = low


def pick_owned(spot_ref, owner_ref, own_ref, one_ref, two_ref, three_ref, out_ref):
    here = spot_ref[0]
    out_ref[...] = jnp.zeros_like(out_ref)
    for step, ref in enumerate((own_ref, one_ref, two_ref, three_ref)):
        block = jnp.maximum(here - step, 0)
        mine = (here >= step) & (owner_ref[block] == here)
        rank = rank_of(owner_ref, block)

        @pl.when(mine)
        def _():
            out_ref[rank] = ref[...]


def rotate(g0, g1, g2, g3, cols_ref, rights_ref, first_ref, second_ref, new_first_ref, new_second_ref, tail_ref):
    for slot in range(CAP):
        gradient = jnp.concatenate([g[slot] for g in (g0, g1, g2, g3)], axis=0)
        inner = jnp.dot(cols_ref[0, slot], gradient, preferred_element_type=f32)
        inner = inner + jnp.dot(cols_ref[1, slot], gradient, preferred_element_type=f32)
        inner = inner.astype(bf16)
        rotated = jnp.dot(inner, rights_ref[0, slot], preferred_element_type=f32)
        rotated = rotated + jnp.dot(inner, rights_ref[1, slot], preferred_element_type=f32)
        new_first = beta_first * first_ref[slot] + (1.0 - beta_first) * rotated
        new_second = beta_second * second_ref[slot] + (1.0 - beta_second) * rotated * rotated
        new_first_ref[slot] = new_first
        new_second_ref[slot] = new_second
        direction = (new_first / (jnp.sqrt(new_second) + epsilon)).astype(bf16)
        across = (((1,), (1,)), ((), ()))
        tail = lax.dot_general(direction, rights_ref[0, slot], across, preferred_element_type=f32)
        tail = tail + lax.dot_general(direction, rights_ref[1, slot], across, preferred_element_type=f32)
        tail_ref[slot] = tail.astype(bf16)


def turn_back(spot_ref, owner_ref, t0, t1, t2, t3, rows_ref, out0, out1, out2, out3, turned_ref):
    for slot in range(CAP):
        tail = jnp.concatenate([t[slot] for t in (t0, t1, t2, t3)], axis=0)
        turned = jnp.dot(rows_ref[0, slot], tail, preferred_element_type=f32)
        turned = turned + jnp.dot(rows_ref[1, slot], tail, preferred_element_type=f32)
        turned_ref[slot] = turned.astype(bf16)
    here = spot_ref[0]
    for step, out in enumerate((out0, out1, out2, out3)):
        out[...] = turned_ref[rank_of(owner_ref, jnp.maximum(here - step, 0))]


def pick_update(spot_ref, owner_ref, own_ref, one_ref, two_ref, three_ref, out_ref):
    here = spot_ref[0]
    offset = owner_ref[here] - here
    for step, ref in enumerate((own_ref, one_ref, two_ref, three_ref)):

        @pl.when(offset == step)
        def _():
            out_ref[...] = ref[...]


def struct(shape, dtype):
    return jax.ShapeDtypeStruct(shape, dtype)


def per_device(grad_rows, owner_list, basis_left, basis_right, first_moment, second_moment):
    slots, order, width = basis_left.shape
    part = grad_rows.shape[1]
    spot = jnp.stack([lax.axis_index("owner"), lax.axis_index("shard")]).astype(jnp.int32)
    params = pltpu.CompilerParams(vmem_limit_bytes=40 * 1024 * 1024)

    own = grad_rows[0]
    arrived = [shifted(own, "owner", step, False) for step in range(1, REACH)]

    cols, rows, rights = pl.pallas_call(
        prepare,
        out_shape=(
            struct((2, slots, part, order), bf16),
            struct((2, slots, part, order), bf16),
            struct((2, slots, order, order), bf16),
        ),
        in_specs=[SMEM, VMEM, VMEM],
        out_specs=(VMEM, VMEM, VMEM),
        compiler_params=params,
        cost_estimate=pl.CostEstimate(flops=4_000_000, bytes_accessed=8 << 20, transcendentals=0),
        name="prepare",
    )(spot, basis_left, basis_right)

    owned = pl.pallas_call(
        pick_owned,
        out_shape=struct((slots, part, width), bf16),
        in_specs=[SMEM, SMEM] + [VMEM] * 4,
        out_specs=VMEM,
        compiler_params=params,
        name="pick_owned",
    )(spot, owner_list, own, *arrived)

    peers = [shifted(owned, "shard", step, True) for step in range(1, 4)]

    new_first, new_second, tail = pl.pallas_call(
        rotate,
        out_shape=(
            struct((slots, part, width), f32),
            struct((slots, part, width), f32),
            struct((slots, part, width), bf16),
        ),
        in_specs=[VMEM] * 8,
        out_specs=(VMEM, VMEM, VMEM),
        compiler_params=params,
        name="rotate",
    )(owned, *peers, cols, rights, first_moment, second_moment)

    tails = [shifted(tail, "shard", step, True) for step in range(1, 4)]

    turned = pl.pallas_call(
        turn_back,
        out_shape=tuple(struct((part, width), bf16) for _ in range(REACH)),
        in_specs=[SMEM, SMEM] + [VMEM] * 5,
        out_specs=(VMEM,) * REACH,
        scratch_shapes=[pltpu.VMEM((slots, part, width), bf16)],
        compiler_params=params,
        name="turn_back",
    )(spot, owner_list, tail, *tails, rows)

    returned = [shifted(turned[step], "owner", -step, False) for step in range(1, REACH)]

    update = pl.pallas_call(
        pick_update,
        out_shape=struct((part, width), bf16),
        in_specs=[SMEM, SMEM] + [VMEM] * 4,
        out_specs=VMEM,
        compiler_params=params,
        name="pick_update",
    )(spot, owner_list, turned[0], *returned)
    return update[None], new_first, new_second


def solution(mesh):
    in_specs = (
        P("owner", "shard", None),
        P(),
        P("owner", None, None),
        P("owner", None, None),
        P("owner", "shard", None),
        P("owner", "shard", None),
    )
    out_specs = (P("owner", "shard", None), P("owner", "shard", None), P("owner", "shard", None))
    return jax.shard_map(
        per_device, mesh=mesh, in_specs=in_specs, out_specs=out_specs, check_vma=False
    )
```

```python
import jax
import jax.numpy as jnp
from jax import lax
from jax.experimental import pallas as pl
from jax.experimental.pallas import tpu as pltpu
from jax.sharding import PartitionSpec as P

REACH = 4
CAP = 2
PEERS = 4

beta_first = 0.9
beta_second = 0.999
epsilon = 1e-08
bf16 = jnp.bfloat16
f32 = jnp.float32
VMEM = pl.BlockSpec(memory_space=pltpu.VMEM)
SMEM = pl.BlockSpec(memory_space=pltpu.SMEM)
params = pltpu.CompilerParams(vmem_limit_bytes=40 * 1024 * 1024)


def shifted(x, axis, by, wrap):
    devices = lax.axis_size(axis)
    if wrap:
        pairs = [(i, (i + by) % devices) for i in range(devices)]
    else:
        pairs = [(i, i + by) for i in range(devices) if 0 <= i + by < devices]
    return lax.ppermute(x, axis, pairs)


def from_opposite(x):
    return lax.ppermute(x, "shard", [(i, PEERS - 1 - i) for i in range(PEERS)])


def rank_of(owner_ref, block):
    before = owner_ref[jnp.maximum(block - 1, 0)]
    return ((block > 0) & (before == owner_ref[block])).astype(jnp.int32)


def worked_slot(shard):
    return lax.div(shard, CAP)


def before(shard, step):
    return lax.rem(shard + PEERS - step, PEERS)


def after(shard, step):
    return lax.rem(shard + step, PEERS)


def split(x):
    high = x.astype(bf16)
    return high, (x - high.astype(f32)).astype(bf16)


def narrow(spot_ref, owner_ref, own_ref, first_ref, second_ref, out_ref, copy_ref, plan_ref):
    here, shard = spot_ref[0], spot_ref[1]
    for step in range(REACH):
        block = jnp.maximum(here - step, 0)
        mine = (here >= step) & (owner_ref[block] == here)
        rank = rank_of(owner_ref, block)
        plan_ref[step] = jnp.where(mine, rank, CAP)
        plan_ref[REACH + step] = rank
    plan_ref[2 * REACH] = owner_ref[here] - here
    plan_ref[2 * REACH + 1] = shard
    slot = 1 - worked_slot(shard)
    out_ref[0] = first_ref[slot].astype(bf16)
    out_ref[1] = second_ref[slot].astype(bf16)
    copy_ref[...] = own_ref[...]


def prepare(spot_ref, left_ref, right_ref, turn_ref, back_ref, rights_ref):
    shard = spot_ref[1]
    slot = worked_slot(shard)
    part = turn_ref.shape[0] // 2
    at = lambda place: pl.ds(pl.multiple_of(place * part, part), part)
    for i, columns in enumerate((at(shard), at(PEERS - 1 - shard))):
        here = slice(i * part, (i + 1) * part)
        for step in range(PEERS):
            there = slice(step * part, (step + 1) * part)
            turn_ref[here, there] = left_ref[slot, at(before(shard, step)), columns].astype(bf16).T
            high, low = split(left_ref[slot, at(after(shard, step)), columns])
            back_ref[0, there, here] = high
            back_ref[1, there, here] = low
    high, low = split(right_ref[slot])
    rights_ref[0] = high
    rights_ref[1] = low


def pick_owned(plan_ref, own_ref, one_ref, two_ref, three_ref, *out_refs):
    shard = plan_ref[2 * REACH + 1]
    for step, out_ref in enumerate(out_refs):
        wanted = worked_slot(after(shard, step))
        out_ref[...] = jnp.zeros_like(out_ref)
        for hop, ref in enumerate((own_ref, one_ref, two_ref, three_ref)):

            @pl.when(plan_ref[hop] == wanted)
            def _():
                out_ref[...] = ref[...]


def moved(first, second, rotated):
    new_first = beta_first * first + (1.0 - beta_first) * rotated
    new_second = beta_second * second + (1.0 - beta_second) * rotated * rotated
    return new_first, new_second


def advance(
    plan_ref, g0, g1, g2, g3, moments_ref, turn_ref, back_ref, rights_ref, first_ref, second_ref,
    mine_ref, theirs_ref, keep_ref, send1, send2, send3,
):
    part = first_ref.shape[1]
    slot = worked_slot(plan_ref[2 * REACH + 1])
    gradient = jnp.concatenate([g[...] for g in (g0, g1, g2, g3)], axis=0)
    inner = jnp.dot(turn_ref[...], gradient, preferred_element_type=f32).astype(bf16)
    rotated = jnp.dot(inner, rights_ref[0], preferred_element_type=f32)
    rotated = rotated + jnp.dot(inner, rights_ref[1], preferred_element_type=f32)
    mine_ref[...] = rotated[:part]
    theirs_ref[...] = rotated[part:].astype(bf16)
    first = jnp.concatenate([first_ref[slot], moments_ref[0].astype(f32)], axis=0)
    second = jnp.concatenate([second_ref[slot], moments_ref[1].astype(f32)], axis=0)
    new_first, new_second = moved(first, second, rotated)
    direction = (new_first / (jnp.sqrt(new_second) + epsilon)).astype(bf16)
    across = (((1,), (1,)), ((), ()))
    tail = lax.dot_general(direction, rights_ref[0], across, preferred_element_type=f32)
    tail = tail + lax.dot_general(direction, rights_ref[1], across, preferred_element_type=f32)
    tail = tail.astype(bf16)
    turned = jnp.dot(back_ref[0], tail, preferred_element_type=f32)
    turned = turned + jnp.dot(back_ref[1], tail, preferred_element_type=f32)
    keep_ref[...] = turned[:part]
    for step, send in enumerate((send1, send2, send3), 1):
        send[...] = turned[step * part : (step + 1) * part].astype(bf16)


def add_parts(plan_ref, p0, p1, p2, p3, out0, out1, out2, out3, sum_ref):
    shard = plan_ref[2 * REACH + 1]
    sum_ref[...] = jnp.zeros_like(sum_ref)
    for step, ref in enumerate((p0, p1, p2, p3)):
        slot = worked_slot(before(shard, step))
        sum_ref[slot] = sum_ref[slot] + ref[...].astype(f32)
    for step, out in enumerate((out0, out1, out2, out3)):
        out[...] = sum_ref[plan_ref[REACH + step]].astype(bf16)


def finish(plan_ref, mine_ref, theirs_ref, first_ref, second_ref, new_first_ref, new_second_ref):
    slot = worked_slot(plan_ref[2 * REACH + 1])
    for place, rotated in ((slot, mine_ref[...]), (1 - slot, theirs_ref[...].astype(f32))):
        new_first, new_second = moved(first_ref[place], second_ref[place], rotated)
        new_first_ref[place] = new_first
        new_second_ref[place] = new_second


def pick_update(plan_ref, own_ref, one_ref, two_ref, three_ref, out_ref):
    offset = plan_ref[2 * REACH]
    for step, ref in enumerate((own_ref, one_ref, two_ref, three_ref)):

        @pl.when(offset == step)
        def _():
            out_ref[...] = ref[...]


def struct(shape, dtype):
    return jax.ShapeDtypeStruct(shape, dtype)


def cost(flops, moved_bytes):
    return pl.CostEstimate(flops=flops, bytes_accessed=moved_bytes, transcendentals=0)


def per_device(grad_rows, owner_list, basis_left, basis_right, first_moment, second_moment):
    slots, order, width = basis_left.shape
    part = grad_rows.shape[1]
    rows = struct((part, width), bf16)
    wide_rows = struct((part, width), f32)
    spot = jnp.stack([lax.axis_index("owner"), lax.axis_index("shard")]).astype(jnp.int32)

    own = grad_rows[0]
    arrived = [shifted(own, "owner", step, False) for step in range(1, REACH)]

    narrowed, own_copy, plan = pl.pallas_call(
        narrow,
        out_shape=(struct((2, part, width), bf16), rows, struct((16,), jnp.int32)),
        in_specs=[SMEM, SMEM] + [VMEM] * 3,
        out_specs=(VMEM, VMEM, SMEM),
        compiler_params=params,
        cost_estimate=cost(0, 3 << 19),
        name="narrow",
    )(spot, owner_list, own, first_moment, second_moment)
    moments = from_opposite(narrowed)

    turn, back, rights = pl.pallas_call(
        prepare,
        out_shape=(
            struct((2 * part, order), bf16),
            struct((2, order, 2 * part), bf16),
            struct((2, order, order), bf16),
        ),
        in_specs=[SMEM, VMEM, VMEM],
        out_specs=(VMEM, VMEM, VMEM),
        compiler_params=params,
        cost_estimate=cost(4_000_000, 8 << 20),
        name="prepare",
    )(spot, basis_left, basis_right)

    owned = pl.pallas_call(
        pick_owned,
        out_shape=(rows,) * PEERS,
        in_specs=[SMEM] + [VMEM] * 4,
        out_specs=(VMEM,) * PEERS,
        compiler_params=params,
        cost_estimate=cost(50_000_000_000, 1 << 20),
        name="pick_owned",
    )(plan, own_copy, *arrived)

    gathered = [owned[0]] + [shifted(owned[step], "shard", step, True) for step in range(1, PEERS)]

    mine, theirs, keep, *sends = pl.pallas_call(
        advance,
        out_shape=(wide_rows, rows, wide_rows, rows, rows, rows),
        in_specs=[SMEM] + [VMEM] * 10,
        out_specs=(VMEM,) * 6,
        compiler_params=params,
        name="advance",
    )(plan, *gathered, moments, turn, back, rights, first_moment, second_moment)

    parts = [keep] + [shifted(sends[step - 1], "shard", step, True) for step in range(1, PEERS)]
    theirs = from_opposite(theirs)

    turned = pl.pallas_call(
        add_parts,
        out_shape=(rows,) * REACH,
        in_specs=[SMEM] + [VMEM] * 4,
        out_specs=(VMEM,) * REACH,
        scratch_shapes=[pltpu.VMEM((slots, part, width), f32)],
        compiler_params=params,
        name="add_parts",
    )(plan, *parts)

    returned = [shifted(turned[step], "owner", -step, False) for step in range(1, REACH)]

    new_first, new_second = pl.pallas_call(
        finish,
        out_shape=(struct((slots, part, width), f32),) * 2,
        in_specs=[SMEM] + [VMEM] * 4,
        out_specs=(VMEM,) * 2,
        compiler_params=params,
        cost_estimate=cost(1_000_000, 2 << 20),
        name="finish",
    )(plan, mine, theirs, first_moment, second_moment)

    update = pl.pallas_call(
        pick_update,
        out_shape=rows,
        in_specs=[SMEM] + [VMEM] * 4,
        out_specs=VMEM,
        compiler_params=params,
        name="pick_update",
    )(plan, turned[0], *returned)
    return update[None], new_first, new_second


def solution(mesh):
    in_specs = (
        P("owner", "shard", None),
        P(),
        P("owner", None, None),
        P("owner", None, None),
        P("owner", "shard", None),
        P("owner", "shard", None),
    )
    out_specs = (P("owner", "shard", None), P("owner", "shard", None), P("owner", "shard", None))
    return jax.shard_map(
        per_device, mesh=mesh, in_specs=in_specs, out_specs=out_specs, check_vma=False
    )
```

```python
import jax
import jax.numpy as jnp
from jax import lax
from jax.experimental import pallas as pl
from jax.experimental.pallas import tpu as pltpu
from jax.sharding import PartitionSpec as P

REACH = 4
CAP = 2
PEERS = 4

beta_first = 0.9
beta_second = 0.999
epsilon = 1e-08
bf16 = jnp.bfloat16
f32 = jnp.float32
VMEM = pl.BlockSpec(memory_space=pltpu.VMEM)
SMEM = pl.BlockSpec(memory_space=pltpu.SMEM)
ANY = pl.BlockSpec(memory_space=pl.ANY)
params = pltpu.CompilerParams(vmem_limit_bytes=40 * 1024 * 1024)


def moved_on(x, by):
    devices = lax.axis_size("owner")
    return lax.ppermute(x, "owner", [(i, i + by) for i in range(devices) if 0 <= i + by < devices])


def from_neighbour(x):
    return lax.ppermute(x, "shard", [(i, i ^ 1) for i in range(PEERS)])


def from_partner(x):
    return lax.ppermute(x, "shard", [(i, 3 - i) for i in range(PEERS)])


def from_far(x):
    return lax.ppermute(x, "shard", [(i, i ^ 2) for i in range(PEERS)])


def worked_slot(shard):
    return lax.rem(lax.div(shard + 1, 2), 2)


def column_order(shard):
    odd = lax.rem(shard, 2)
    return shard, shard + 1 - 2 * odd, PEERS - 1 - shard, lax.rem(shard + 2, PEERS)


def split(x):
    high = x.astype(bf16)
    return high, (x - high.astype(f32)).astype(bf16)


def prepare(spot_ref, left_ref, right_ref, turn_ref, back_ref, rights_ref):
    shard = spot_ref[1]
    slot = worked_slot(shard)
    part = turn_ref.shape[0] // 2
    places = [pl.ds(pl.multiple_of(place * part, part), part) for place in column_order(shard)]
    for i, columns in enumerate(places[:2]):
        here = slice(i * part, (i + 1) * part)
        for k, rows in enumerate(places):
            there = slice(k * part, (k + 1) * part)
            block = left_ref[slot, rows, columns]
            high, low = split(block)
            turn_ref[here, there] = high.T
            back_ref[0, there, here] = high
            back_ref[1, there, here] = low
    high, low = split(right_ref[slot])
    rights_ref[0] = high
    rights_ref[1] = low


def stage(spot_ref, owner_ref, own_ref, copy_ref, plan_ref):
    here = spot_ref[0]
    slot = worked_slot(spot_ref[1])
    for step in range(REACH):
        block = jnp.maximum(here - step, 0)
        owned = (here >= step) & (owner_ref[block] == here)
        rank = ((block > 0) & (owner_ref[jnp.maximum(block - 1, 0)] == owner_ref[block])).astype(jnp.int32)
        plan_ref[step] = jnp.where(owned, (rank != slot).astype(jnp.int32), 2)
        plan_ref[REACH + step] = rank
    plan_ref[2 * REACH] = owner_ref[here] - here
    copy_ref[...] = own_ref[...]


def pick_owned(plan_ref, own_ref, one_ref, two_ref, three_ref, mine_ref, theirs_ref):
    for which, out_ref in enumerate((mine_ref, theirs_ref)):
        out_ref[...] = jnp.zeros_like(out_ref)
        for step, ref in enumerate((own_ref, one_ref, two_ref, three_ref)):

            @pl.when(plan_ref[step] == which)
            def _():
                out_ref[...] = ref[...]


def moved(first, second, rotated):
    new_first = beta_first * first + (1.0 - beta_first) * rotated
    new_second = beta_second * second + (1.0 - beta_second) * rotated * rotated
    return new_first, new_second


def advance(
    spot_ref, partner_ref, far_ref, neighbour_ref, own_ref, moments_ref, turn_ref, back_ref, rights_ref,
    first_ref, second_ref, mine_ref, keep_ref, to_neighbour, to_partner, to_far,
):
    part = first_ref.shape[1]
    slot = worked_slot(spot_ref[1])
    gradient = jnp.concatenate([g[...] for g in (own_ref, neighbour_ref, partner_ref, far_ref)], axis=0)
    inner = jnp.dot(turn_ref[...], gradient, preferred_element_type=f32).astype(bf16)
    rotated = jnp.dot(inner, rights_ref[0], preferred_element_type=f32)
    rotated = rotated + jnp.dot(inner, rights_ref[1], preferred_element_type=f32)
    mine_ref[...] = rotated[:part]
    to_neighbour[1] = rotated[part:].astype(bf16)
    first = jnp.concatenate([first_ref[slot], moments_ref[0].astype(f32)], axis=0)
    second = jnp.concatenate([second_ref[slot], moments_ref[1].astype(f32)], axis=0)
    new_first, new_second = moved(first, second, rotated)
    direction = (new_first / (jnp.sqrt(new_second) + epsilon)).astype(bf16)
    across = (((1,), (1,)), ((), ()))
    tail = lax.dot_general(direction, rights_ref[0], across, preferred_element_type=f32)
    tail = tail + lax.dot_general(direction, rights_ref[1], across, preferred_element_type=f32)
    tail = tail.astype(bf16)
    turned = jnp.dot(back_ref[0], tail, preferred_element_type=f32)
    turned = turned + jnp.dot(back_ref[1], tail, preferred_element_type=f32)
    keep_ref[...] = turned[:part]
    for step, send in enumerate((to_neighbour.at[0], to_partner, to_far), 1):
        send[...] = turned[step * part : (step + 1) * part].astype(bf16)


def add_parts(
    spot_ref, plan_ref, partner_ref, far_ref, neighbour_ref, keep_ref, out0, out1, out2, out3, sum_ref
):
    slot = worked_slot(spot_ref[1])
    sum_ref[slot] = (keep_ref[...] + partner_ref[...].astype(f32)).astype(bf16)
    sum_ref[1 - slot] = (neighbour_ref[0].astype(f32) + far_ref[...].astype(f32)).astype(bf16)
    for step, out in enumerate((out0, out1, out2, out3)):
        out[...] = sum_ref[plan_ref[REACH + step]]


def finish(spot_ref, mine_ref, theirs_ref, first_ref, second_ref, new_first_ref, new_second_ref):
    slot = worked_slot(spot_ref[1])
    for place, rotated in ((slot, mine_ref[...]), (1 - slot, theirs_ref[1].astype(f32))):
        new_first, new_second = moved(first_ref[place], second_ref[place], rotated)
        new_first_ref[place] = new_first
        new_second_ref[place] = new_second


def pick_update(plan_ref, three_ref, two_ref, one_ref, own_ref, out_ref, sem):
    offset = plan_ref[2 * REACH]
    for step, ref in enumerate((own_ref, one_ref, two_ref, three_ref)):

        @pl.when(offset == step)
        def _():
            copy = pltpu.make_async_copy(ref, out_ref, sem)
            copy.start()
            copy.wait()


def struct(shape, dtype):
    return jax.ShapeDtypeStruct(shape, dtype)


def cost(flops, moved_bytes):
    return pl.CostEstimate(flops=flops, bytes_accessed=moved_bytes, transcendentals=0)


def per_device(grad_rows, owner_list, basis_left, basis_right, first_moment, second_moment):
    slots, order, width = basis_left.shape
    part = grad_rows.shape[1]
    rows = struct((part, width), bf16)
    wide_rows = struct((part, width), f32)
    here, shard = lax.axis_index("owner"), lax.axis_index("shard")
    spot = jnp.stack([here, shard]).astype(jnp.int32)

    own = grad_rows[0]
    arrived = [moved_on(own, step) for step in range(1, REACH)]

    other_slot = 1 - worked_slot(shard)
    moments = from_neighbour(
        jnp.stack(
            [
                lax.dynamic_index_in_dim(moment, other_slot, 0, keepdims=False).astype(bf16)
                for moment in (first_moment, second_moment)
            ]
        )
    )

    turn, back, rights = pl.pallas_call(
        prepare,
        out_shape=(
            struct((2 * part, order), bf16),
            struct((2, order, 2 * part), bf16),
            struct((2, order, order), bf16),
        ),
        in_specs=[SMEM, VMEM, VMEM],
        out_specs=(VMEM, VMEM, VMEM),
        compiler_params=params,
        cost_estimate=cost(4_000_000, 8 << 20),
        name="prepare",
    )(spot, basis_left, basis_right)

    own_copy, plan = pl.pallas_call(
        stage,
        out_shape=(rows, struct((16,), jnp.int32)),
        in_specs=[SMEM, SMEM, VMEM],
        out_specs=(VMEM, SMEM),
        compiler_params=params,
        name="stage",
    )(spot, owner_list, own)

    owned, others = pl.pallas_call(
        pick_owned,
        out_shape=(rows, rows),
        in_specs=[SMEM] + [VMEM] * 4,
        out_specs=(VMEM, VMEM),
        compiler_params=params,
        cost_estimate=cost(50_000_000_000, 1 << 20),
        name="pick_owned",
    )(plan, own_copy, *arrived)

    mine, keep, to_neighbour, to_partner, to_far = pl.pallas_call(
        advance,
        out_shape=(wide_rows, wide_rows, struct((2, part, width), bf16), rows, rows),
        in_specs=[SMEM] + [VMEM] * 10,
        out_specs=(VMEM,) * 5,
        compiler_params=params,
        name="advance",
    )(
        spot, from_partner(owned), from_far(others), from_neighbour(others), owned, moments, turn, back, rights,
        first_moment, second_moment,
    )

    theirs = from_neighbour(to_neighbour)

    turned = pl.pallas_call(
        add_parts,
        out_shape=(rows,) * REACH,
        in_specs=[SMEM, SMEM] + [VMEM] * 4,
        out_specs=(VMEM,) * REACH,
        scratch_shapes=[pltpu.VMEM((slots, part, width), bf16)],
        compiler_params=params,
        name="add_parts",
    )(spot, plan, from_partner(to_partner), from_far(to_far), theirs, keep)

    returned = [moved_on(turned[step], -step) for step in range(1, REACH)]

    new_first, new_second = pl.pallas_call(
        finish,
        out_shape=(struct((slots, part, width), f32),) * 2,
        in_specs=[SMEM] + [VMEM] * 4,
        out_specs=(VMEM,) * 2,
        compiler_params=params,
        cost_estimate=cost(1_000_000, 2 << 20),
        name="finish",
    )(spot, mine, theirs, first_moment, second_moment)

    update = pl.pallas_call(
        pick_update,
        out_shape=rows,
        in_specs=[SMEM] + [VMEM] * 4,
        out_specs=ANY,
        scratch_shapes=[pltpu.SemaphoreType.DMA],
        compiler_params=params,
        name="pick_update",
    )(plan, *returned[::-1], turned[0])
    return update[None], new_first, new_second


def solution(mesh):
    in_specs = (
        P("owner", "shard", None),
        P(),
        P("owner", None, None),
        P("owner", None, None),
        P("owner", "shard", None),
        P("owner", "shard", None),
    )
    out_specs = (P("owner", "shard", None), P("owner", "shard", None), P("owner", "shard", None))
    return jax.shard_map(
        per_device, mesh=mesh, in_specs=in_specs, out_specs=out_specs, check_vma=False
    )
```

```python
import jax
import jax.numpy as jnp
from jax import lax
from jax.experimental import pallas as pl
from jax.experimental.pallas import tpu as pltpu
from jax.sharding import PartitionSpec as P

REACH = 4
CAP = 2
PEERS = 4

beta_first = 0.9
beta_second = 0.999
epsilon = 1e-08
bf16 = jnp.bfloat16
f32 = jnp.float32
VMEM = pl.BlockSpec(memory_space=pltpu.VMEM)
SMEM = pl.BlockSpec(memory_space=pltpu.SMEM)
ANY = pl.BlockSpec(memory_space=pl.ANY)
params = pltpu.CompilerParams(vmem_limit_bytes=40 * 1024 * 1024)


def moved_on(x, by):
    devices = lax.axis_size("owner")
    return lax.ppermute(x, "owner", [(i, i + by) for i in range(devices) if 0 <= i + by < devices])


def from_neighbour(x):
    return lax.ppermute(x, "shard", [(i, i ^ 1) for i in range(PEERS)])


def moved_round(x, by):
    return lax.ppermute(x, "shard", [(i, (i + by) % PEERS) for i in range(PEERS)])


WORKED = (0, 1, 1, 0)


def worked_slot(shard):
    return lax.rem(lax.div(shard + 1, 2), 2)


def before(shard, step):
    return lax.rem(shard + PEERS - step, PEERS)


def after(shard, step):
    return lax.rem(shard + step, PEERS)


def split(x):
    high = x.astype(bf16)
    return high, (x - high.astype(f32)).astype(bf16)


def prepare(spot_ref, left_ref, right_ref, turn_ref, back_ref, rights_ref):
    shard = spot_ref[1]
    slot = worked_slot(shard)
    part = turn_ref.shape[0] // 2
    at = lambda place: pl.ds(pl.multiple_of(place * part, part), part)
    for i, place in enumerate((shard, shard + 1 - 2 * lax.rem(shard, 2))):
        here = slice(i * part, (i + 1) * part)
        for step in range(PEERS):
            there = slice(step * part, (step + 1) * part)
            turn_ref[here, there] = left_ref[slot, at(before(shard, step)), at(place)].astype(bf16).T
        high, low = split(left_ref[slot, :, at(place)])
        back_ref[0, :, here] = high
        back_ref[1, :, here] = low
    high, low = split(right_ref[slot])
    rights_ref[0] = high
    rights_ref[1] = low


def stage(spot_ref, owner_ref, own_ref, copy_ref, plan_ref):
    here = spot_ref[0]
    for step in range(REACH):
        block = jnp.maximum(here - step, 0)
        owned = (here >= step) & (owner_ref[block] == here)
        rank = ((block > 0) & (owner_ref[jnp.maximum(block - 1, 0)] == owner_ref[block])).astype(jnp.int32)
        plan_ref[step] = jnp.where(owned, rank, CAP)
        plan_ref[REACH + step] = rank
    plan_ref[2 * REACH] = owner_ref[here] - here
    copy_ref[...] = own_ref[...]


def pick_owned(spot_ref, plan_ref, own_ref, one_ref, two_ref, three_ref, *out_refs):
    for ahead, out_ref in enumerate(out_refs):
        wanted = worked_slot(after(spot_ref[1], ahead))
        out_ref[...] = jnp.zeros_like(out_ref)
        for step, ref in enumerate((own_ref, one_ref, two_ref, three_ref)):

            @pl.when(plan_ref[step] == wanted)
            def _():
                out_ref[...] = ref[...]


def moved(first, second, rotated):
    new_first = beta_first * first + (1.0 - beta_first) * rotated
    new_second = beta_second * second + (1.0 - beta_second) * rotated * rotated
    return new_first, new_second


def advance(
    spot_ref, g0, g1, g2, g3, moments_ref, turn_ref, back_ref, rights_ref,
    first_ref, second_ref, mine_ref, theirs_ref, send_ref,
):
    part = first_ref.shape[1]
    slot = worked_slot(spot_ref[1])
    gradient = jnp.concatenate([g[...] for g in (g0, g1, g2, g3)], axis=0)
    inner = jnp.dot(turn_ref[...], gradient, preferred_element_type=f32).astype(bf16)
    rotated = jnp.dot(inner, rights_ref[0], preferred_element_type=f32)
    rotated = rotated + jnp.dot(inner, rights_ref[1], preferred_element_type=f32)
    mine_ref[...] = rotated[:part]
    theirs_ref[...] = rotated[part:].astype(bf16)
    first = jnp.concatenate([first_ref[slot], moments_ref[0].astype(f32)], axis=0)
    second = jnp.concatenate([second_ref[slot], moments_ref[1].astype(f32)], axis=0)
    new_first, new_second = moved(first, second, rotated)
    direction = (new_first / (jnp.sqrt(new_second) + epsilon)).astype(bf16)
    across = (((1,), (1,)), ((), ()))
    tail = lax.dot_general(direction, rights_ref[0], across, preferred_element_type=f32)
    tail = tail + lax.dot_general(direction, rights_ref[1], across, preferred_element_type=f32)
    tail = tail.astype(bf16)
    turned = jnp.dot(back_ref[0], tail, preferred_element_type=f32)
    turned = turned + jnp.dot(back_ref[1], tail, preferred_element_type=f32)
    send_ref[...] = turned.astype(bf16).reshape(send_ref.shape)


def add_parts(plan_ref, parts_ref, out0, out1, out2, out3, sum_ref):
    for slot in range(CAP):
        one, two = [parts_ref[place].astype(f32) for place, worked in enumerate(WORKED) if worked == slot]
        sum_ref[slot] = (one + two).astype(bf16)
    for step, out in enumerate((out0, out1, out2, out3)):
        out[...] = sum_ref[plan_ref[REACH + step]]


def finish(spot_ref, mine_ref, theirs_ref, first_ref, second_ref, new_first_ref, new_second_ref):
    slot = worked_slot(spot_ref[1])
    for place, rotated in ((slot, mine_ref[...]), (1 - slot, theirs_ref[...].astype(f32))):
        new_first, new_second = moved(first_ref[place], second_ref[place], rotated)
        new_first_ref[place] = new_first
        new_second_ref[place] = new_second


def pick_update(plan_ref, three_ref, two_ref, one_ref, own_ref, out_ref, sem):
    offset = plan_ref[2 * REACH]
    for step, ref in enumerate((own_ref, one_ref, two_ref, three_ref)):

        @pl.when(offset == step)
        def _():
            copy = pltpu.make_async_copy(ref, out_ref, sem)
            copy.start()
            copy.wait()


def struct(shape, dtype):
    return jax.ShapeDtypeStruct(shape, dtype)


def cost(flops, moved_bytes):
    return pl.CostEstimate(flops=flops, bytes_accessed=moved_bytes, transcendentals=0)


def per_device(grad_rows, owner_list, basis_left, basis_right, first_moment, second_moment):
    slots, order, width = basis_left.shape
    part = grad_rows.shape[1]
    rows = struct((part, width), bf16)
    wide_rows = struct((part, width), f32)
    here, shard = lax.axis_index("owner"), lax.axis_index("shard")
    spot = jnp.stack([here, shard]).astype(jnp.int32)

    own = grad_rows[0]
    arrived = [moved_on(own, step) for step in range(1, REACH)]

    other_slot = 1 - worked_slot(shard)
    moments = from_neighbour(
        jnp.stack(
            [
                lax.dynamic_index_in_dim(moment, other_slot, 0, keepdims=False).astype(bf16)
                for moment in (first_moment, second_moment)
            ]
        )
    )

    turn, back, rights = pl.pallas_call(
        prepare,
        out_shape=(
            struct((2 * part, order), bf16),
            struct((2, order, 2 * part), bf16),
            struct((2, order, order), bf16),
        ),
        in_specs=[SMEM, VMEM, VMEM],
        out_specs=(VMEM, VMEM, VMEM),
        compiler_params=params,
        cost_estimate=cost(4_000_000, 8 << 20),
        name="prepare",
    )(spot, basis_left, basis_right)

    own_copy, plan = pl.pallas_call(
        stage,
        out_shape=(rows, struct((16,), jnp.int32)),
        in_specs=[SMEM, SMEM, VMEM],
        out_specs=(VMEM, SMEM),
        compiler_params=params,
        name="stage",
    )(spot, owner_list, own)

    owned = pl.pallas_call(
        pick_owned,
        out_shape=(rows,) * PEERS,
        in_specs=[SMEM, SMEM] + [VMEM] * 4,
        out_specs=(VMEM,) * PEERS,
        compiler_params=params,
        cost_estimate=cost(50_000_000_000, 1 << 20),
        name="pick_owned",
    )(spot, plan, own_copy, *arrived)
    gathered = [owned[0]] + [moved_round(owned[ahead], ahead) for ahead in range(1, PEERS)]

    mine, theirs, send = pl.pallas_call(
        advance,
        out_shape=(wide_rows, rows, struct((PEERS, part, width), bf16)),
        in_specs=[SMEM] + [VMEM] * 10,
        out_specs=(VMEM,) * 3,
        compiler_params=params,
        name="advance",
    )(
        spot, *gathered, moments, turn, back, rights,
        first_moment, second_moment,
    )

    parts = lax.all_to_all(send, "shard", 0, 0, tiled=True)

    turned = pl.pallas_call(
        add_parts,
        out_shape=(rows,) * REACH,
        in_specs=[SMEM, VMEM],
        out_specs=(VMEM,) * REACH,
        scratch_shapes=[pltpu.VMEM((slots, part, width), bf16)],
        compiler_params=params,
        name="add_parts",
    )(plan, parts)

    returned = [moved_on(turned[step], -step) for step in range(1, REACH)]

    new_first, new_second = pl.pallas_call(
        finish,
        out_shape=(struct((slots, part, width), f32),) * 2,
        in_specs=[SMEM] + [VMEM] * 4,
        out_specs=(VMEM,) * 2,
        compiler_params=params,
        cost_estimate=cost(1_000_000, 2 << 20),
        name="finish",
    )(spot, mine, from_neighbour(theirs), first_moment, second_moment)

    update = pl.pallas_call(
        pick_update,
        out_shape=rows,
        in_specs=[SMEM] + [VMEM] * 4,
        out_specs=ANY,
        scratch_shapes=[pltpu.SemaphoreType.DMA],
        compiler_params=params,
        name="pick_update",
    )(plan, *returned[::-1], turned[0])
    return update[None], new_first, new_second


def solution(mesh):
    in_specs = (
        P("owner", "shard", None),
        P(),
        P("owner", None, None),
        P("owner", None, None),
        P("owner", "shard", None),
        P("owner", "shard", None),
    )
    out_specs = (P("owner", "shard", None), P("owner", "shard", None), P("owner", "shard", None))
    return jax.shard_map(
        per_device, mesh=mesh, in_specs=in_specs, out_specs=out_specs, check_vma=False
    )
```

```python
import jax
import jax.numpy as jnp
from jax import lax
from jax.experimental import pallas as pl
from jax.experimental.pallas import tpu as pltpu
from jax.sharding import PartitionSpec as P

REACH = 4
CAP = 2
PEERS = 4

beta_first = 0.9
beta_second = 0.999
epsilon = 1e-08
bf16 = jnp.bfloat16
f32 = jnp.float32
VMEM = pl.BlockSpec(memory_space=pltpu.VMEM)
SMEM = pl.BlockSpec(memory_space=pltpu.SMEM)
ANY = pl.BlockSpec(memory_space=pl.ANY)
params = pltpu.CompilerParams(vmem_limit_bytes=40 * 1024 * 1024)


def moved_on(x, by):
    devices = lax.axis_size("owner")
    return lax.ppermute(x, "owner", [(i, i + by) for i in range(devices) if 0 <= i + by < devices])


def from_neighbour(x):
    return lax.ppermute(x, "shard", [(i, i ^ 1) for i in range(PEERS)])


def moved_round(x, by):
    return lax.ppermute(x, "shard", [(i, (i + by) % PEERS) for i in range(PEERS)])


WORKED = (0, 1, 1, 0)


def worked_slot(shard):
    return lax.rem(lax.div(shard + 1, 2), 2)


def before(shard, step):
    return lax.rem(shard + PEERS - step, PEERS)


def after(shard, step):
    return lax.rem(shard + step, PEERS)


def split(x):
    high = x.astype(bf16)
    return high, (x - high.astype(f32)).astype(bf16)


def prepare(spot_ref, left_ref, right_ref, turn_ref, back_ref, rights_ref):
    shard = spot_ref[1]
    slot = worked_slot(shard)
    part = turn_ref.shape[0] // 2
    at = lambda place: pl.ds(pl.multiple_of(place * part, part), part)
    for i, place in enumerate((shard, shard + 1 - 2 * lax.rem(shard, 2))):
        here = slice(i * part, (i + 1) * part)
        for step in range(PEERS):
            there = slice(step * part, (step + 1) * part)
            turn_ref[here, there] = left_ref[slot, at(before(shard, step)), at(place)].astype(bf16).T
        high, low = split(left_ref[slot, :, at(place)])
        back_ref[0, :, here] = high
        back_ref[1, :, here] = low
    high, low = split(right_ref[slot])
    rights_ref[0] = high
    rights_ref[1] = low


def stage(spot_ref, owner_ref, own_ref, copy_ref, plan_ref):
    here = spot_ref[0]
    for step in range(REACH):
        block = jnp.maximum(here - step, 0)
        owned = (here >= step) & (owner_ref[block] == here)
        rank = ((block > 0) & (owner_ref[jnp.maximum(block - 1, 0)] == owner_ref[block])).astype(jnp.int32)
        plan_ref[step] = jnp.where(owned, rank, CAP)
        plan_ref[REACH + step] = rank
    plan_ref[2 * REACH] = owner_ref[here] - here
    copy_ref[...] = own_ref[...]


def pick_owned(spot_ref, plan_ref, own_ref, one_ref, two_ref, three_ref, *out_refs):
    for ahead, out_ref in enumerate(out_refs):
        wanted = worked_slot(after(spot_ref[1], ahead))
        out_ref[...] = jnp.zeros_like(out_ref)
        for step, ref in enumerate((own_ref, one_ref, two_ref, three_ref)):

            @pl.when(plan_ref[step] == wanted)
            def _():
                out_ref[...] = ref[...]


def moved(first, second, rotated):
    new_first = beta_first * first + (1.0 - beta_first) * rotated
    new_second = beta_second * second + (1.0 - beta_second) * rotated * rotated
    return new_first, new_second


def advance(
    spot_ref, g0, g2, g3, g1, moments_ref, turn_ref, back_ref, rights_ref,
    first_ref, second_ref, mine_ref, theirs_ref, send_ref,
):
    part = first_ref.shape[1]
    slot = worked_slot(spot_ref[1])
    gradient = jnp.concatenate([g[...] for g in (g0, g1, g2, g3)], axis=0)
    inner = jnp.dot(turn_ref[...], gradient, preferred_element_type=f32).astype(bf16)
    rotated = jnp.dot(inner, rights_ref[0], preferred_element_type=f32)
    rotated = rotated + jnp.dot(inner, rights_ref[1], preferred_element_type=f32)
    mine_ref[...] = rotated[:part]
    theirs_ref[...] = rotated[part:].astype(bf16)
    first = jnp.concatenate([first_ref[slot], moments_ref[0].astype(f32)], axis=0)
    second = jnp.concatenate([second_ref[slot], moments_ref[1].astype(f32)], axis=0)
    new_first, new_second = moved(first, second, rotated)
    direction = (new_first / (jnp.sqrt(new_second) + epsilon)).astype(bf16)
    across = (((1,), (1,)), ((), ()))
    tail = lax.dot_general(direction, rights_ref[0], across, preferred_element_type=f32)
    tail = tail + lax.dot_general(direction, rights_ref[1], across, preferred_element_type=f32)
    tail = tail.astype(bf16)
    turned = jnp.dot(back_ref[0], tail, preferred_element_type=f32)
    turned = turned + jnp.dot(back_ref[1], tail, preferred_element_type=f32)
    send_ref[...] = turned.astype(bf16).reshape(send_ref.shape)


def add_parts(plan_ref, parts_ref, out0, out1, out2, out3, sum_ref):
    for slot in range(CAP):
        one, two = [parts_ref[place].astype(f32) for place, worked in enumerate(WORKED) if worked == slot]
        sum_ref[slot] = (one + two).astype(bf16)
    for step, out in enumerate((out0, out1, out2, out3)):
        out[...] = sum_ref[plan_ref[REACH + step]]


def finish(spot_ref, mine_ref, theirs_ref, first_ref, second_ref, new_first_ref, new_second_ref):
    slot = worked_slot(spot_ref[1])
    for place, rotated in ((slot, mine_ref[...]), (1 - slot, theirs_ref[...].astype(f32))):
        new_first, new_second = moved(first_ref[place], second_ref[place], rotated)
        new_first_ref[place] = new_first
        new_second_ref[place] = new_second


def pick_update(plan_ref, three_ref, two_ref, one_ref, own_ref, out_ref, sem):
    offset = plan_ref[2 * REACH]
    for step, ref in enumerate((own_ref, one_ref, two_ref, three_ref)):

        @pl.when(offset == step)
        def _():
            copy = pltpu.make_async_copy(ref, out_ref, sem)
            copy.start()
            copy.wait()


def struct(shape, dtype):
    return jax.ShapeDtypeStruct(shape, dtype)


def cost(flops, moved_bytes):
    return pl.CostEstimate(flops=flops, bytes_accessed=moved_bytes, transcendentals=0)


def per_device(grad_rows, owner_list, basis_left, basis_right, first_moment, second_moment):
    slots, order, width = basis_left.shape
    part = grad_rows.shape[1]
    rows = struct((part, width), bf16)
    wide_rows = struct((part, width), f32)
    here, shard = lax.axis_index("owner"), lax.axis_index("shard")
    spot = jnp.stack([here, shard]).astype(jnp.int32)

    own = grad_rows[0]
    arrived = [moved_on(own, step) for step in range(1, REACH)]

    other_slot = 1 - worked_slot(shard)
    moments = from_neighbour(
        jnp.stack(
            [
                lax.dynamic_index_in_dim(moment, other_slot, 0, keepdims=False).astype(bf16)
                for moment in (first_moment, second_moment)
            ]
        )
    )

    turn, back, rights = pl.pallas_call(
        prepare,
        out_shape=(
            struct((2 * part, order), bf16),
            struct((2, order, 2 * part), bf16),
            struct((2, order, order), bf16),
        ),
        in_specs=[SMEM, VMEM, VMEM],
        out_specs=(VMEM, VMEM, VMEM),
        compiler_params=params,
        cost_estimate=cost(4_000_000, 8 << 20),
        name="prepare",
    )(spot, basis_left, basis_right)

    own_copy, plan = pl.pallas_call(
        stage,
        out_shape=(rows, struct((16,), jnp.int32)),
        in_specs=[SMEM, SMEM, VMEM],
        out_specs=(VMEM, SMEM),
        compiler_params=params,
        name="stage",
    )(spot, owner_list, own)

    owned = pl.pallas_call(
        pick_owned,
        out_shape=(rows,) * PEERS,
        in_specs=[SMEM, SMEM] + [VMEM] * 4,
        out_specs=(VMEM,) * PEERS,
        compiler_params=params,
        cost_estimate=cost(50_000_000_000, 1 << 20),
        name="pick_owned",
    )(spot, plan, own_copy, *arrived)
    gathered = [owned[0]] + [moved_round(owned[ahead], ahead) for ahead in range(1, PEERS)]

    mine, theirs, send = pl.pallas_call(
        advance,
        out_shape=(wide_rows, rows, struct((PEERS, part, width), bf16)),
        in_specs=[SMEM] + [VMEM] * 10,
        out_specs=(VMEM,) * 3,
        compiler_params=params,
        name="advance",
    )(
        spot, gathered[0], gathered[2], gathered[3], gathered[1], moments, turn, back, rights,
        first_moment, second_moment,
    )

    parts = lax.all_to_all(send, "shard", 0, 0, tiled=True)

    turned = pl.pallas_call(
        add_parts,
        out_shape=(rows,) * REACH,
        in_specs=[SMEM, VMEM],
        out_specs=(VMEM,) * REACH,
        scratch_shapes=[pltpu.VMEM((slots, part, width), bf16)],
        compiler_params=params,
        name="add_parts",
    )(plan, parts)

    returned = [moved_on(turned[step], -step) for step in range(1, REACH)]

    new_first, new_second = pl.pallas_call(
        finish,
        out_shape=(struct((slots, part, width), f32),) * 2,
        in_specs=[SMEM] + [VMEM] * 4,
        out_specs=(VMEM,) * 2,
        compiler_params=params,
        cost_estimate=cost(1_000_000, 2 << 20),
        name="finish",
    )(spot, mine, from_neighbour(theirs), first_moment, second_moment)

    update = pl.pallas_call(
        pick_update,
        out_shape=rows,
        in_specs=[SMEM] + [VMEM] * 4,
        out_specs=ANY,
        scratch_shapes=[pltpu.SemaphoreType.DMA],
        compiler_params=params,
        name="pick_update",
    )(plan, *returned[::-1], turned[0])
    return update[None], new_first, new_second


def solution(mesh):
    in_specs = (
        P("owner", "shard", None),
        P(),
        P("owner", None, None),
        P("owner", None, None),
        P("owner", "shard", None),
        P("owner", "shard", None),
    )
    out_specs = (P("owner", "shard", None), P("owner", "shard", None), P("owner", "shard", None))
    return jax.shard_map(
        per_device, mesh=mesh, in_specs=in_specs, out_specs=out_specs, check_vma=False
    )
```
